256 devices in a mesh: bld: 32 (over x, z), tm: 8 (over y, core).
Axes of the slice: x: 4, y: 4, z: 8, core: 2. Of those that a mesh axis runs over, the one named last changes fastest.
Arguments:
- power: float32 [32768, 2048], P('bld', 'tm'), may hold values from 0.05 to 3.9, as said below
- base_temp: float32 [32768, 2048], P('bld', 'tm'), may hold values from -8 to 8
- band_low: float32 [8, 2048], P(None, 'tm'), may hold values from -1.2 to -0.3
- band_high: float32 [8, 2048], P(None, 'tm'), may hold values from 0.3 to 1.2
- kernels: bfloat16 [4, 256], replicated, as said below
- gains: float32 [32768, 4], P('bld'), may hold values from 0.3 to 3
- zones: int32 [32768], P('bld'), may hold values from 1 to 4
- plan_class: int32 [32768], P('bld'), may hold values from 0 to 7
- duals: float32 [2048], P('tm'), may hold values from -2 to 2
Outputs:
- power_out: float32 [32768, 2048], P('bld', 'tm')
- duals_out: float32 [2048], P('tm')
The draws below stay inside these ranges and needn't reach their ends.
Inputs may be any that keep to these rules, and one draw needn't show every extreme that they name: power of a building lies between 0.05 and 3.9. Impulse kernels are nonnegative.
All inputs are finite; a program needn't handle non-finite values.
Results may differ from the reference program's by a relative error of at most 0.00069.
Values may be sent and summed in bfloat16 or wider, within the bound.
A program may use at most 64 MiB of HBM per device.

```python
import math
import jax
import jax.numpy as jnp
from jax import lax

B_DEV = 1024
TAPS = 256
ZMAX = 4
SCHED = 8
ITERS = 2
NB = 32768
HORIZON = 2048
N_BLD = 32


def draw_power(key, part):
    key = jax.random.fold_in(key, 11)
    ramp = 1.0 + 2.0 * jnp.arange(NB, dtype=jnp.float32) / (NB - 1)
    values = jax.random.uniform(key, (NB, HORIZON), jnp.float32, 0.2, 1.0)
    return ramp[:, None] * values


def draw_kernels(key, part):
    key = jax.random.fold_in(key, 23)
    key_tau, key_rough = jax.random.split(key)
    tau = jnp.exp(jax.random.uniform(key_tau, (ZMAX,), jnp.float32, jnp.log(10.0), jnp.log(400.0)))
    rough = jax.random.uniform(key_rough, (ZMAX, TAPS), jnp.float32, 0.5, 1.5)
    lags = jnp.arange(TAPS, dtype=jnp.float32)
    amp = 1.0 / (tau * (1.0 - jnp.exp(-TAPS / tau)))
    values = amp[:, None] * jnp.exp(-lags[None, :] / tau[:, None]) * rough
    return values.astype(jnp.bfloat16)


def touch_ends(result, stream_key, smallest, top_value):
    longest = result.shape.index(max(result.shape))
    spots = []
    for shift in (0, 1):
        where = [jax.random.randint(jax.random.fold_in(stream_key, axis), (), 0, length) for axis, length in enumerate(result.shape)]
        where[longest] = (where[longest] + shift) % result.shape[longest]
        spots.append(tuple(where))
    return result.at[spots[0]].set(smallest).at[spots[1]].set(top_value)


def block_levels(stream_key, extent, pieces, least, high):
    level = 1.0
    for axis_at, shards_of in pieces:
        draws = jax.random.uniform(jax.random.fold_in(jax.random.fold_in(stream_key, 6), axis_at), (shards_of,), jnp.float32, least / len(pieces), high / len(pieces))
        level = level * jnp.repeat(jnp.exp(draws), extent[axis_at] // shards_of).reshape((-1,) + (1,) * (len(extent) - 1 - axis_at))
    return level


def bell_draw(key, shape, width, reach, shards=(), held_as=jnp.bfloat16):
    factor_of = block_levels(key, shape, shards, -0.22, 0.18) if shards else 1.0
    drawn = jax.random.normal(key, shape, jnp.float32) * width * factor_of
    return jnp.minimum(jnp.maximum(drawn, -reach), reach).astype(held_as)


def setup_inputs(seed: int = 0) -> dict:
    arg_keys = jax.random.split(jax.random.key(seed), 10)
    power = draw_power(jax.random.fold_in(arg_keys[9], 71), 0)
    base_temp = bell_draw(arg_keys[1], (NB, HORIZON), 1.5, 8.0, ((0, 32), (1, 8)), jnp.float32)
    band_low = jnp.clip(-1.2 + 0.90000004 * jax.random.uniform(arg_keys[2], (SCHED, HORIZON), jnp.float32) ** block_levels(arg_keys[2], (SCHED, HORIZON), ((1, 8),), -0.2, 0.2), -1.2, -0.3)
    band_high = jnp.clip(0.3 + 0.90000004 * jax.random.uniform(arg_keys[3], (SCHED, HORIZON), jnp.float32) ** block_levels(arg_keys[3], (SCHED, HORIZON), ((1, 8),), -0.2, 0.2), 0.3, 1.2)
    kernels = draw_kernels(jax.random.fold_in(arg_keys[9], 71), 0)
    gains = jnp.clip(jnp.exp(math.log(3.0) - 2.3025851 * jax.random.uniform(arg_keys[5], (NB, ZMAX), jnp.float32) ** block_levels(arg_keys[5], (NB, ZMAX), ((0, 32),), -0.2, 0.2)), 0.3, 3.0)
    zones = touch_ends(jax.random.randint(arg_keys[6], (NB,), 1, ZMAX + 1), jax.random.fold_in(arg_keys[6], 1), 1, ZMAX).astype(jnp.int32)
    plan_class = touch_ends(jax.random.randint(arg_keys[7], (NB,), 0, SCHED), jax.random.fold_in(arg_keys[7], 1), 0, SCHED - 1).astype(jnp.int32)
    duals = bell_draw(arg_keys[8], (HORIZON,), 0.3, 2.0, ((0, 8),), jnp.float32)
    return {"power": power, "base_temp": base_temp, "band_low": band_low, "band_high": band_high, "kernels": kernels, "gains": gains, "zones": zones, "plan_class": plan_class, "duals": duals}


def reference(power, base_temp, band_low, band_high, kernels, gains, zones, plan_class, duals):
    length = HORIZON + TAPS
    kern = kernels.astype(jnp.float32)
    kspec = jnp.fft.rfft(kern, length)
    slots = jnp.arange(ZMAX, dtype=jnp.int32)
    mask = (slots[None, :] < zones[:, None]).astype(jnp.float32)
    weight = gains * mask

    def grad_block(items):
        u_blk, base_blk, gain_blk, weight_blk, class_blk = items
        packed = lax.optimization_barrier(u_blk.astype(jnp.bfloat16)).astype(jnp.float32)
        spec = jnp.fft.rfft(packed, length)[:, None, :] * kspec[None]
        response = jnp.fft.irfft(spec, length)[..., :HORIZON]
        theta = base_blk[:, None, :] - gain_blk[:, :, None] * response
        low = band_low[class_blk][:, None, :]
        high = band_high[class_blk][:, None, :]
        excess = weight_blk[:, :, None] * (theta - jnp.clip(theta, low, high))
        excess = lax.optimization_barrier(excess.astype(jnp.bfloat16)).astype(jnp.float32)
        back = jnp.fft.rfft(excess, length) * jnp.conj(kspec)[None]
        pull = jnp.fft.irfft(back, length)[..., :HORIZON]
        return -jnp.sum(pull, axis=1)

    blocks = (
        base_temp.reshape(N_BLD, B_DEV, HORIZON),
        gains.reshape(N_BLD, B_DEV, ZMAX),
        weight.reshape(N_BLD, B_DEV, ZMAX),
        plan_class.reshape(N_BLD, B_DEV),
    )
    u_now = power
    y_now = duals
    for step in range(ITERS):
        fleet = jnp.sum(u_now, axis=0)
        peak = jnp.max(fleet)
        ratio = fleet / peak
        price = y_now + 1.0 * ratio
        grad = lax.map(grad_block, (u_now.reshape(N_BLD, B_DEV, HORIZON),) + blocks)
        grad = grad.reshape(NB, HORIZON)
        u_now = jnp.clip(u_now - 0.5 * (grad + price[None, :]), 0.0, 4.0)
        y_now = y_now + 1.0 * (ratio - 0.5)
    return u_now, y_now
```

```python
import functools

import jax
import jax.numpy as jnp
from jax import lax
from jax.experimental import pallas as pl
from jax.experimental.pallas import tpu as pltpu
from jax.sharding import PartitionSpec as P

ITERS = 2
ROWS = 128
MESH = pl.DeviceIdType.MESH
CODE = 32767.0


def split3(value):
    top = value.astype(jnp.bfloat16)
    rest = value - top.astype(jnp.float32)
    mid = rest.astype(jnp.bfloat16)
    low = (rest - mid.astype(jnp.float32)).astype(jnp.bfloat16)
    return [top, mid, low]


def kernel(
    nz,
    nx,
    nt,
    power,
    base,
    band_low,
    band_high,
    kernels,
    gains,
    zones,
    classes,
    duals,
    out,
    duals_out,
    u_now,
    base_vm,
    over,
    under,
    own,
    packed,
    halo_u,
    code_out,
    code_in,
    forward,
    adjoint,
    bands,
    onehot,
    cols,
    sums,
    part_z,
    part_x,
    part_t,
    load_sem,
    u_send,
    u_recv,
    p_send,
    p_recv,
    r_send,
    r_recv,
):
    count, steps = u_now.shape
    zcount = kernels.shape[0]
    chunks = count // ROWS
    bld = lax.axis_index("bld")
    tm = lax.axis_index("tm")
    x, z = bld // nz, lax.rem(bld, nz)
    right = (bld, lax.rem(tm + 1, nt))
    left = (bld, lax.rem(tm + nt - 1, nt))
    peers_z = [(x * nz + lax.rem(z + k, nz), tm) for k in range(1, nz)]
    peers_x = [(lax.rem(x + k, nx) * nz + z, tm) for k in range(1, nx)]
    peers_t = [(bld, lax.rem(tm + k, nt)) for k in range(1, nt)]

    def rows(c):
        return pl.ds(pl.multiple_of(c * ROWS, ROWS), ROWS)

    def load(which, c):
        source, target = ((power, u_now), (base, base_vm))[which]
        return pltpu.make_async_copy(
            source.at[rows(c)], target.at[rows(c)], load_sem.at[which, c]
        )

    def u_copy(it, c):
        return pltpu.make_async_remote_copy(
            src_ref=packed.at[it, rows(c)],
            dst_ref=halo_u.at[it, rows(c)],
            send_sem=u_send.at[it, c],
            recv_sem=u_recv.at[it, c],
            device_id=right,
            device_id_type=MESH,
        )

    def p_copy(it, c):
        return pltpu.make_async_remote_copy(
            src_ref=code_out.at[it, rows(c)],
            dst_ref=code_in.at[it, rows(c)],
            send_sem=p_send.at[it, c],
            recv_sem=p_recv.at[it, c],
            device_id=left,
            device_id_type=MESH,
        )

    stages = ((part_z, peers_z, z, 0), (part_x, peers_x, x, nz), (part_t, peers_t, tm, nz + nx))

    def part_copy(it, stage, k):
        buf, peers, mine, first = stages[stage]
        return pltpu.make_async_remote_copy(
            src_ref=buf.at[it, mine],
            dst_ref=buf.at[it, mine],
            send_sem=r_send.at[it, first + k],
            recv_sem=r_recv.at[it, first + k],
            device_id=peers[k - 1],
            device_id_type=MESH,
        )

    def stage_send(it, stage, value):
        buf, peers, mine, _ = stages[stage]
        buf[it, mine] = value
        for k in range(1, len(peers) + 1):
            part_copy(it, stage, k).start()

    def stage_wait(it, stage):
        buf, peers, _, _ = stages[stage]
        for k in range(1, len(peers) + 1):
            part_copy(it, stage, k).wait_recv()
        return buf[it]

    def send_local(it):
        stage_send(it, 0, jnp.sum(sums[it], axis=0, keepdims=True))

    def send_rows(it):
        stage_send(it, 1, jnp.sum(stage_wait(it, 0), axis=0))

    def send_peak(it):
        fleet = jnp.sum(stage_wait(it, 1), axis=0)
        top = jnp.max(fleet, axis=1, keepdims=True)
        stage_send(it, 2, jnp.broadcast_to(top, (1, 128)))

    def ratio(it):
        fleet = jnp.sum(part_x[it], axis=0)
        top = jnp.max(stage_wait(it, 2), axis=0)[:, :1]
        return fleet / top

    for c in range(chunks):
        load(0, c).start()
    for c in range(chunks):
        load(1, c).start()

    barrier = pltpu.get_barrier_semaphore()
    for peer in peers_z + peers_x + peers_t:
        pl.semaphore_signal(barrier, inc=1, device_id=peer, device_id_type=MESH)

    sums[...] = jnp.zeros_like(sums)

    def pack(c, carry):
        load(0, c).wait()
        value = u_now[rows(c)]
        packed[0, rows(c)] = value.astype(jnp.bfloat16)
        sums[0] += jnp.sum(value.reshape(ROWS // 8, 8, steps), axis=0)
        return carry

    lax.fori_loop(0, chunks, pack, 0)
    pl.semaphore_wait(barrier, len(peers_z + peers_x + peers_t))
    send_local(0)

    def send_first(c, carry):
        u_copy(0, c).start()
        return carry

    lax.fori_loop(0, chunks, send_first, 0)

    kern = kernels[...].astype(jnp.float32)
    at_row = lax.broadcasted_iota(jnp.int32, (steps, steps), 0)
    at_col = lax.broadcasted_iota(jnp.int32, (steps, steps), 1)
    edge = jnp.where(tm > 0, 0, steps)
    for slot in range(zcount):
        wide = jnp.broadcast_to(kern[slot : slot + 1], (steps, steps))
        ring = pltpu.roll(wide, 0, 1, stride=1, stride_axis=0)
        place = pl.ds(slot * steps, steps)
        forward[:steps, place] = jnp.where(at_row - at_col > edge, ring, 0.0).astype(jnp.bfloat16)
        forward[steps:, place] = jnp.where(at_row <= at_col, ring, 0.0).astype(jnp.bfloat16)
        ring = ring.T
        adjoint[place, :steps] = jnp.where(at_row >= at_col, ring, 0.0).astype(jnp.bfloat16)
        adjoint[place, steps:] = jnp.where(at_col - at_row > edge, ring, 0.0).astype(jnp.bfloat16)

    gain = gains[...]
    slots = lax.broadcasted_iota(jnp.int32, (zcount, count), 0)
    weight = jnp.where(slots < zones[...], gain, 0.0)
    total = jnp.sum(kern, axis=1, keepdims=True)
    bound = 1.01 * jnp.sum(weight * total * (8.0 + 4.0 * gain * total), axis=0, keepdims=True)
    bound = jnp.maximum(bound, 1e-20)
    scale_in = bound / (CODE * CODE)
    scale_out = (CODE * CODE) / bound
    none = jnp.zeros((6, count), jnp.float32)
    cols[...] = jnp.concatenate([gain, weight, scale_out, scale_in, none], axis=0).T
    nsched = band_low.shape[0]
    plans = lax.broadcasted_iota(jnp.int32, (nsched, count), 0)
    chosen = jnp.where(plans == classes[...], 1.0, 0.0)
    onehot[...] = jnp.concatenate([chosen] * 3, axis=0).T.astype(jnp.bfloat16)
    lows, highs = split3(band_low[...]), split3(band_high[...])
    bands[...] = jnp.concatenate(
        [jnp.concatenate([lo, hi], axis=1).astype(jnp.float32) for lo, hi in zip(lows, highs)],
        axis=0,
    ).astype(jnp.bfloat16)

    def excess_and_pull(it, c):
        col = cols[rows(c)]
        window = jnp.concatenate([halo_u[it, rows(c)], packed[it, rows(c)]], axis=1)
        hi, lo = over[rows(c)], under[rows(c)]
        parts = []
        for slot in range(zcount):
            place = pl.ds(slot * steps, steps)
            response = jnp.dot(window, forward[:, place], preferred_element_type=jnp.float32)
            change = col[:, slot : slot + 1] * response
            far = jnp.maximum(hi - change, jnp.minimum(lo - change, 0.0))
            scale = col[:, zcount + slot : zcount + slot + 1]
            parts.append((scale * far).astype(jnp.bfloat16))
        excess = jnp.concatenate(parts, axis=1)
        pull = jnp.dot(excess, adjoint[...], preferred_element_type=jnp.float32)
        own[rows(c)] = pull[:, :steps]
        sent = pull[:, steps:]
        size = jnp.sqrt(jnp.abs(sent) * col[:, 2 * zcount : 2 * zcount + 1])
        code = jnp.round(jnp.where(sent < 0.0, -size, size))
        code_out[it, rows(c)] = jnp.clip(code, -CODE, CODE).astype(jnp.int16)

    def updated(it, c, price):
        p_copy(it, c).wait_recv()
        code = code_in[it, rows(c)].astype(jnp.float32)
        scale = cols[rows(c)][:, 2 * zcount + 1 : 2 * zcount + 2]
        pull = own[rows(c)] + code * jnp.abs(code) * scale
        return jnp.clip(u_now[rows(c)] - 0.5 * (price - pull), 0.0, 4.0)

    def first(c):
        load(1, c).wait()
        limits = jnp.dot(onehot[rows(c)], bands[...], preferred_element_type=jnp.float32)
        value = base_vm[rows(c)]
        under[rows(c)] = value - limits[:, :steps]
        over[rows(c)] = value - limits[:, steps:]
        u_copy(0, c).wait_recv()
        excess_and_pull(0, c)
        p_copy(0, c).start()

    def second(c):
        u_copy(1, c).wait_recv()
        excess_and_pull(1, c)
        p_copy(1, c).start()

    def between(c, price):
        value = updated(0, c, price)
        u_now[rows(c)] = value
        packed[1, rows(c)] = value.astype(jnp.bfloat16)
        sums[1] += jnp.sum(value.reshape(ROWS // 8, 8, steps), axis=0)
        u_copy(1, c).start()

    send_rows(0)
    first(0)
    send_peak(0)
    first(1)
    now = ratio(0)
    price = duals[...] + 1.0 * now
    y_now = duals[...] + 1.0 * (now - 0.5)

    def middle(c, carry):
        first(c)
        between(c - 2, price)
        return carry

    lax.fori_loop(2, chunks, middle, 0)
    between(chunks - 2, price)
    between(chunks - 1, price)
    send_local(1)
    second(0)
    send_rows(1)
    second(1)
    send_peak(1)

    def last(c, carry):
        second(c)
        return carry

    lax.fori_loop(2, chunks, last, 0)
    now = ratio(1)
    price = y_now + 1.0 * now
    duals_out[...] = y_now + 1.0 * (now - 0.5)

    def finish(c, carry):
        out[rows(c)] = updated(1, c, price)
        return carry

    lax.fori_loop(0, chunks, finish, 0)

    for it in range(ITERS):
        for c in range(chunks):
            u_copy(it, c).wait_send()
            p_copy(it, c).wait_send()
        for stage in range(3):
            for k in range(1, len(stages[stage][1]) + 1):
                part_copy(it, stage, k).wait_send()


def body(nz, nx, nt, power, base, band_low, band_high, kernels, gains, zones, classes, duals):
    count, steps = power.shape
    zcount = kernels.shape[0]
    chunks = count // ROWS
    nsched = band_low.shape[0]
    vmem = pl.BlockSpec(memory_space=pltpu.VMEM)
    anywhere = pl.BlockSpec(memory_space=pl.ANY)
    f32, bf16 = jnp.float32, jnp.bfloat16
    whole = pltpu.VMEM((count, steps), f32)
    parts = nz + nx + nt
    out, duals_out = pl.pallas_call(
        functools.partial(kernel, nz, nx, nt),
        out_shape=(
            jax.ShapeDtypeStruct((count, steps), f32),
            jax.ShapeDtypeStruct((1, steps), f32),
        ),
        in_specs=[anywhere] * 2 + [vmem] * 7,
        out_specs=(vmem, vmem),
        scratch_shapes=[
            whole,
            whole,
            whole,
            whole,
            whole,
            pltpu.VMEM((ITERS, count, steps), bf16),
            pltpu.VMEM((ITERS, count, steps), bf16),
            pltpu.VMEM((ITERS, count, steps), jnp.int16),
            pltpu.VMEM((ITERS, count, steps), jnp.int16),
            pltpu.VMEM((2 * steps, zcount * steps), bf16),
            pltpu.VMEM((zcount * steps, 2 * steps), bf16),
            pltpu.VMEM((3 * nsched, 2 * steps), bf16),
            pltpu.VMEM((count, 3 * nsched), bf16),
            pltpu.VMEM((count, 16), f32),
            pltpu.VMEM((ITERS, 8, steps), f32),
            pltpu.VMEM((ITERS, nz, 1, steps), f32),
            pltpu.VMEM((ITERS, nx, 1, steps), f32),
            pltpu.VMEM((ITERS, nt, 1, 128), f32),
            pltpu.SemaphoreType.DMA((2, chunks)),
            pltpu.SemaphoreType.DMA((ITERS, chunks)),
            pltpu.SemaphoreType.DMA((ITERS, chunks)),
            pltpu.SemaphoreType.DMA((ITERS, chunks)),
            pltpu.SemaphoreType.DMA((ITERS, chunks)),
            pltpu.SemaphoreType.DMA((ITERS, parts)),
            pltpu.SemaphoreType.DMA((ITERS, parts)),
        ],
        compiler_params=pltpu.CompilerParams(
            collective_id=0, has_side_effects=True, vmem_limit_bytes=40 * 1024 * 1024
        ),
    )(
        power,
        base,
        band_low,
        band_high,
        kernels,
        gains.T,
        zones[None, :],
        classes[None, :],
        duals[None, :],
    )
    return out, duals_out[0]


def solution(mesh):
    in_specs = (
        P("bld", "tm"),
        P("bld", "tm"),
        P(None, "tm"),
        P(None, "tm"),
        P(),
        P("bld", None),
        P("bld"),
        P("bld"),
        P("tm"),
    )
    out_specs = (P("bld", "tm"), P("tm"))
    nz = 8 if mesh.shape["bld"] % 8 == 0 else 1
    nx = mesh.shape["bld"] // nz
    return jax.shard_map(
        functools.partial(body, nz, nx, mesh.shape["tm"]),
        mesh=mesh,
        in_specs=in_specs,
        out_specs=out_specs,
        check_vma=False,
    )
```

```python
import functools

import jax
import jax.numpy as jnp
from jax import lax
from jax.experimental import pallas as pl
from jax.experimental.pallas import tpu as pltpu
from jax.sharding import PartitionSpec as P

ITERS = 2
ROWS = 128
MESH = pl.DeviceIdType.MESH
CODE = 32767.0


def split3(value):
    top = value.astype(jnp.bfloat16)
    rest = value - top.astype(jnp.float32)
    mid = rest.astype(jnp.bfloat16)
    low = (rest - mid.astype(jnp.float32)).astype(jnp.bfloat16)
    return [top, mid, low]


def spread(distances):
    return sorted(range(1, len(distances)), key=lambda k: -distances[k])


def around(k, n):
    return min(k, n - k)


def kernel(
    nz,
    nx,
    nt,
    power,
    base,
    band_low,
    band_high,
    kernels,
    gains,
    zones,
    classes,
    duals,
    out,
    duals_out,
    low_vm,
    high_vm,
    kern_vm,
    gains_vm,
    zones_vm,
    classes_vm,
    duals_vm,
    u_now,
    over,
    under,
    own,
    packed,
    halo_u,
    code_out,
    code_in,
    forward,
    adjoint,
    onehot,
    cols,
    part_a,
    part_b,
    load_sem,
    u_send,
    u_recv,
    p_send,
    p_recv,
    r_send,
    r_recv,
):
    count, steps = u_now.shape
    zcount = kernels.shape[0]
    copies = count // ROWS
    ny = nt // 2
    bld = lax.axis_index("bld")
    tm = lax.axis_index("tm")
    x, z = bld // nz, lax.rem(bld, nz)
    y, core = tm // 2, lax.rem(tm, 2)
    right = (bld, lax.rem(tm + 1, nt))
    left = (bld, lax.rem(tm + nt - 1, nt))

    far_a = spread([2 * around(k // 2, nz) + k % 2 for k in range(2 * nz)])
    far_b = spread([around(k // ny, nx) + around(k % ny, ny) for k in range(nx * ny)])
    peers_a = [
        (x * nz + lax.rem(z + k // 2, nz), 2 * y + lax.rem(core + k % 2, 2)) for k in far_a
    ]
    peers_b = [
        (lax.rem(x + k // ny, nx) * nz + z, 2 * lax.rem(y + k % ny, ny) + core) for k in far_b
    ]
    stages = ((part_a, peers_a, 2 * z + core), (part_b, peers_b, x * ny + y))

    small = (
        (gains, gains_vm),
        (zones, zones_vm),
        (classes, classes_vm),
        (kernels, kern_vm),
        (band_low, low_vm),
        (band_high, high_vm),
        (duals, duals_vm),
    )
    half = count // 2
    loads = [
        pltpu.make_async_copy(power.at[pl.ds(0, half)], u_now.at[pl.ds(0, half)], load_sem.at[0]),
        pltpu.make_async_copy(power.at[pl.ds(half, half)], u_now.at[pl.ds(half, half)], load_sem.at[1]),
        pltpu.make_async_copy(base, under, load_sem.at[2]),
    ] + [
        pltpu.make_async_copy(source, target, load_sem.at[3 + i])
        for i, (source, target) in enumerate(small)
    ]

    def u_copy(it, at, size):
        return pltpu.make_async_remote_copy(
            src_ref=packed.at[it, pl.ds(at, size)],
            dst_ref=halo_u.at[it, pl.ds(at, size)],
            send_sem=u_send.at[it],
            recv_sem=u_recv.at[it, at // ROWS],
            device_id=right,
            device_id_type=MESH,
        )

    def p_copy(it, at, size):
        return pltpu.make_async_remote_copy(
            src_ref=code_out.at[it, pl.ds(at, size)],
            dst_ref=code_in.at[it, pl.ds(at, size)],
            send_sem=p_send.at[it],
            recv_sem=p_recv.at[it, at // ROWS],
            device_id=left,
            device_id_type=MESH,
        )

    def part_send(it, stage, value):
        buf, peers, mine = stages[stage]
        buf[it, mine] = value
        for peer in peers:
            pltpu.make_async_remote_copy(
                src_ref=buf.at[it, mine],
                dst_ref=buf.at[it, mine],
                send_sem=r_send.at[it, stage],
                recv_sem=r_recv.at[it, stage],
                device_id=peer,
                device_id_type=MESH,
            ).start()

    def part_all(it, stage):
        buf, peers, _ = stages[stage]
        return pltpu.make_async_remote_copy(
            src_ref=buf.at[it, pl.ds(0, len(peers))],
            dst_ref=buf.at[it, pl.ds(0, len(peers))],
            send_sem=r_send.at[it, stage],
            recv_sem=r_recv.at[it, stage],
            device_id=peers[0],
            device_id_type=MESH,
        )

    def send_local(it, sums):
        part_send(it, 0, jnp.sum(sums, axis=0, keepdims=True))

    def send_pair(it):
        part_all(it, 0).wait_recv()
        slots = part_a[it].reshape(nz, 2, 1, steps)
        part_send(it, 1, jnp.sum(slots, axis=0))

    def ratio(it):
        part_all(it, 1).wait_recv()
        fleet = jnp.sum(part_b[it].reshape(nx, ny, 2, steps), axis=0)
        top = jnp.max(fleet, axis=(0, 1, 2), keepdims=True)[0, 0]
        mine = part_b[it, y, core]
        for k in range(1, nx):
            mine = mine + part_b[it, k * ny + y, core]
        return mine / top

    for load in loads:
        load.start()

    barrier = pltpu.get_barrier_semaphore()
    others = peers_a + peers_b + [left, right]
    for peer in others:
        pl.semaphore_signal(barrier, inc=1, device_id=peer, device_id_type=MESH)

    def fold(value):
        return jnp.sum(value.reshape(value.shape[0] // 8, 8, steps), axis=0)

    sums = jnp.zeros((8, steps), jnp.float32)
    for i in range(2):
        loads[i].wait()
        value = u_now[pl.ds(i * half, half)]
        packed[0, pl.ds(i * half, half)] = value.astype(jnp.bfloat16)
        sums = sums + fold(value)
    sums_first = sums
    for load in loads[3:]:
        load.wait()

    kern = kern_vm[...].astype(jnp.float32)
    gain = gains_vm[...]
    slots = lax.broadcasted_iota(jnp.int32, (zcount, count), 0)
    weight = jnp.where(slots < zones_vm[...], gain, 0.0)
    total = jnp.sum(kern, axis=1, keepdims=True)
    bound = 1.01 * jnp.sum(weight * total * (8.0 + 4.0 * gain * total), axis=0, keepdims=True)
    bound = jnp.maximum(bound, 1e-20)
    scale_in = bound / (CODE * CODE)
    scale_out = (CODE * CODE) / bound
    none = jnp.zeros((6, count), jnp.float32)
    cols[...] = jnp.concatenate([gain, weight, scale_out, scale_in, none], axis=0).T
    nsched = band_low.shape[0]
    plans = lax.broadcasted_iota(jnp.int32, (nsched, count), 0)
    chosen = jnp.where(plans == classes_vm[...], 1.0, 0.0)
    onehot[...] = jnp.concatenate([chosen] * 3, axis=0).T.astype(jnp.bfloat16)

    pl.semaphore_wait(barrier, len(others))
    send_local(0, sums_first)
    for at in range(0, count, ROWS):
        u_copy(0, at, ROWS).start()

    at_row = lax.broadcasted_iota(jnp.int32, (steps, steps), 0)
    at_col = lax.broadcasted_iota(jnp.int32, (steps, steps), 1)
    edge = jnp.where(tm > 0, 0, steps)
    for slot in range(zcount):
        wide = jnp.broadcast_to(kern[slot : slot + 1], (steps, steps))
        ring = pltpu.roll(wide, 0, 1, stride=1, stride_axis=0)
        place = pl.ds(slot * steps, steps)
        forward[:steps, place] = jnp.where(at_row - at_col > edge, ring, 0.0).astype(jnp.bfloat16)
        forward[steps:, place] = jnp.where(at_row <= at_col, ring, 0.0).astype(jnp.bfloat16)
        ring = ring.T
        adjoint[place, :steps] = jnp.where(at_row >= at_col, ring, 0.0).astype(jnp.bfloat16)
        adjoint[place, steps:] = jnp.where(at_col - at_row > edge, ring, 0.0).astype(jnp.bfloat16)

    lows, highs = split3(low_vm[...]), split3(high_vm[...])
    bands = jnp.concatenate(
        [jnp.concatenate([lo, hi], axis=1).astype(jnp.float32) for lo, hi in zip(lows, highs)],
        axis=0,
    ).astype(jnp.bfloat16)
    loads[2].wait()
    for at in range(0, count, half):
        rows = pl.ds(at, half)
        limits = jnp.dot(onehot[rows], bands, preferred_element_type=jnp.float32)
        value = under[rows]
        under[rows] = value - limits[:, :steps]
        over[rows] = value - limits[:, steps:]

    def excess_and_pull(it, at, size):
        for part in range(at, at + size, ROWS):
            u_copy(it, part, ROWS).wait_recv()
        rows = pl.ds(at, size)
        col = cols[rows]
        window = jnp.concatenate([halo_u[it, rows], packed[it, rows]], axis=1)
        hi, lo = over[rows], under[rows]
        parts = []
        for slot in range(zcount):
            place = pl.ds(slot * steps, steps)
            response = jnp.dot(window, forward[:, place], preferred_element_type=jnp.float32)
            change = col[:, slot : slot + 1] * response
            far = jnp.maximum(hi - change, jnp.minimum(lo - change, 0.0))
            scale = col[:, zcount + slot : zcount + slot + 1]
            parts.append((scale * far).astype(jnp.bfloat16))
        excess = jnp.concatenate(parts, axis=1)
        pull = jnp.dot(excess, adjoint[...], preferred_element_type=jnp.float32)
        own[rows] = pull[:, :steps]
        sent = pull[:, steps:]
        length = jnp.sqrt(jnp.abs(sent) * col[:, 2 * zcount : 2 * zcount + 1])
        code = jnp.round(jnp.where(sent < 0.0, -length, length))
        code_out[it, rows] = jnp.clip(code, -CODE, CODE).astype(jnp.int16)
        for part in range(at, at + size, ROWS):
            p_copy(it, part, ROWS).start()

    def free_part(it, at, size, y_now):
        for part in range(at, at + size, ROWS):
            p_copy(it, part, ROWS).wait_recv()
        rows = pl.ds(at, size)
        code = code_in[it, rows].astype(jnp.float32)
        scale = cols[rows][:, 2 * zcount + 1 : 2 * zcount + 2]
        pull = own[rows] + code * jnp.abs(code) * scale
        return u_now[rows] - 0.5 * (y_now - pull)

    y_now = duals_vm[...]
    places = [(0, 256), (256, 256), (512, 256), (768, 128), (896, 128)]
    assert places[-1][0] + places[-1][1] == count

    excess_and_pull(0, *places[0])
    send_pair(0)
    for place in places[1:]:
        excess_and_pull(0, *place)
    now = ratio(0)
    share = 0.5 * now
    sums = jnp.zeros((8, steps), jnp.float32)
    for at in range(0, count, ROWS):
        rows = pl.ds(at, ROWS)
        value = jnp.clip(free_part(0, at, ROWS, y_now) - share, 0.0, 4.0)
        u_now[rows] = value
        packed[1, rows] = value.astype(jnp.bfloat16)
        sums = sums + fold(value)
        u_copy(1, at, ROWS).start()
    send_local(1, sums)
    y_now = y_now + 1.0 * (now - 0.5)

    excess_and_pull(1, *places[0])
    excess_and_pull(1, *places[1])
    send_pair(1)
    for place in places[2:]:
        excess_and_pull(1, *place)
    for at, size in places:
        own[pl.ds(at, size)] = free_part(1, at, size, y_now)
    now = ratio(1)
    share = 0.5 * now
    duals_out[...] = y_now + 1.0 * (now - 0.5)
    out[...] = jnp.clip(own[...] - share, 0.0, 4.0)

    for it in range(ITERS):
        u_copy(it, 0, count).wait_send()
        p_copy(it, 0, count).wait_send()
        for stage in range(2):
            part_all(it, stage).wait_send()


def body(nz, nx, nt, power, base, band_low, band_high, kernels, gains, zones, classes, duals):
    count, steps = power.shape
    zcount = kernels.shape[0]
    copies = count // ROWS
    nsched = band_low.shape[0]
    vmem = pl.BlockSpec(memory_space=pltpu.VMEM)
    hbm = pl.BlockSpec(memory_space=pltpu.HBM)
    f32, bf16 = jnp.float32, jnp.bfloat16
    whole = pltpu.VMEM((count, steps), f32)
    args = (
        power,
        base,
        band_low,
        band_high,
        kernels,
        gains.T,
        zones[None, :],
        classes[None, :],
        duals[None, :],
    )
    out, duals_out = pl.pallas_call(
        functools.partial(kernel, nz, nx, nt),
        out_shape=(
            jax.ShapeDtypeStruct((count, steps), f32),
            jax.ShapeDtypeStruct((1, steps), f32),
        ),
        in_specs=[hbm] * len(args),
        out_specs=(vmem, vmem),
        scratch_shapes=[pltpu.VMEM(arg.shape, arg.dtype) for arg in args[2:]]
        + [
            whole,
            whole,
            whole,
            whole,
            pltpu.VMEM((ITERS, count, steps), bf16),
            pltpu.VMEM((ITERS, count, steps), bf16),
            pltpu.VMEM((ITERS, count, steps), jnp.int16),
            pltpu.VMEM((ITERS, count, steps), jnp.int16),
            pltpu.VMEM((2 * steps, zcount * steps), bf16),
            pltpu.VMEM((zcount * steps, 2 * steps), bf16),
            pltpu.VMEM((count, 3 * nsched), bf16),
            pltpu.VMEM((count, 16), f32),
            pltpu.VMEM((ITERS, 2 * nz, 1, steps), f32),
            pltpu.VMEM((ITERS, nx * nt // 2, 2, 1, steps), f32),
            pltpu.SemaphoreType.DMA((3 + len(args) - 2,)),
            pltpu.SemaphoreType.DMA((ITERS,)),
            pltpu.SemaphoreType.DMA((ITERS, copies)),
            pltpu.SemaphoreType.DMA((ITERS,)),
            pltpu.SemaphoreType.DMA((ITERS, copies)),
            pltpu.SemaphoreType.DMA((ITERS, 2)),
            pltpu.SemaphoreType.DMA((ITERS, 2)),
        ],
        compiler_params=pltpu.CompilerParams(
            collective_id=0, has_side_effects=True, vmem_limit_bytes=40 * 1024 * 1024
        ),
    )(*[pltpu.with_memory_space_constraint(arg, pltpu.HBM) for arg in args])
    return out, duals_out[0]


def solution(mesh):
    in_specs = (
        P("bld", "tm"),
        P("bld", "tm"),
        P(None, "tm"),
        P(None, "tm"),
        P(),
        P("bld", None),
        P("bld"),
        P("bld"),
        P("tm"),
    )
    out_specs = (P("bld", "tm"), P("tm"))
    nz = 8 if mesh.shape["bld"] % 8 == 0 else 1
    nx = mesh.shape["bld"] // nz
    return jax.shard_map(
        functools.partial(body, nz, nx, mesh.shape["tm"]),
        mesh=mesh,
        in_specs=in_specs,
        out_specs=out_specs,
        check_vma=False,
    )
```

```python
import functools

import jax
import jax.numpy as jnp
from jax import lax
from jax.experimental import pallas as pl
from jax.experimental.pallas import tpu as pltpu
from jax.sharding import PartitionSpec as P

ITERS = 2
ROWS = 128
MESH = pl.DeviceIdType.MESH
CODE = 32767.0
TOP = 4.0
LEAD = 5
LAG = 5


def split3(value):
    top = value.astype(jnp.bfloat16)
    rest = value - top.astype(jnp.float32)
    mid = rest.astype(jnp.bfloat16)
    low = (rest - mid.astype(jnp.float32)).astype(jnp.bfloat16)
    return [top, mid, low]


def spread(distances):
    return sorted(range(1, len(distances)), key=lambda k: -distances[k])


def around(k, n):
    return min(k, n - k)


def kernel(
    nz,
    nx,
    nt,
    power,
    base,
    band_low,
    band_high,
    kernels,
    gains,
    zones,
    classes,
    duals,
    out,
    duals_out,
    low_vm,
    high_vm,
    kern_vm,
    gains_vm,
    zones_vm,
    classes_vm,
    duals_vm,
    u_now,
    over,
    under,
    own,
    packed,
    halo_u,
    code_out,
    code_in,
    free_out,
    free_in,
    forward,
    adjoint,
    onehot,
    cols,
    part_a,
    part_b,
    load_sem,
    u_send,
    u_recv,
    p_send,
    p_recv,
    r_send,
    r_recv,
):
    count, steps = u_now.shape
    zcount = kernels.shape[0]
    copies = count // ROWS
    ny = nt // 2
    bld = lax.axis_index("bld")
    tm = lax.axis_index("tm")
    x, z = bld // nz, lax.rem(bld, nz)
    y, core = tm // 2, lax.rem(tm, 2)
    right = (bld, lax.rem(tm + 1, nt))
    left = (bld, lax.rem(tm + nt - 1, nt))

    far_a = spread([2 * around(k // 2, nz) + k % 2 for k in range(2 * nz)])
    far_b = spread([around(k // ny, nx) + around(k % ny, ny) for k in range(nx * ny)])
    peers_a = [
        (x * nz + lax.rem(z + k // 2, nz), 2 * y + lax.rem(core + k % 2, 2)) for k in far_a
    ]
    peers_b = [
        (lax.rem(x + k // ny, nx) * nz + z, 2 * lax.rem(y + k % ny, ny) + core) for k in far_b
    ]
    stages = ((part_a, peers_a, 2 * z + core), (part_b, peers_b, x * ny + y))

    small = (
        (gains, gains_vm),
        (zones, zones_vm),
        (classes, classes_vm),
        (kernels, kern_vm),
        (band_low, low_vm),
        (band_high, high_vm),
        (duals, duals_vm),
    )
    half = count // 2
    loads = [
        pltpu.make_async_copy(power.at[pl.ds(0, half)], u_now.at[pl.ds(0, half)], load_sem.at[0]),
        pltpu.make_async_copy(power.at[pl.ds(half, half)], u_now.at[pl.ds(half, half)], load_sem.at[1]),
        pltpu.make_async_copy(base, under, load_sem.at[2]),
    ] + [
        pltpu.make_async_copy(source, target, load_sem.at[3 + i])
        for i, (source, target) in enumerate(small)
    ]

    def u_copy(it, at, size):
        source, target = ((packed.at[0], halo_u), (free_out, free_in))[it]
        return pltpu.make_async_remote_copy(
            src_ref=source.at[pl.ds(at, size)],
            dst_ref=target.at[pl.ds(at, size)],
            send_sem=u_send.at[it],
            recv_sem=u_recv.at[it, at // ROWS],
            device_id=right,
            device_id_type=MESH,
        )

    def p_copy(it, at, size):
        return pltpu.make_async_remote_copy(
            src_ref=code_out.at[it, pl.ds(at, size)],
            dst_ref=code_in.at[it, pl.ds(at, size)],
            send_sem=p_send.at[it],
            recv_sem=p_recv.at[it, at // ROWS],
            device_id=left,
            device_id_type=MESH,
        )

    def part_send(it, stage, value):
        buf, peers, mine = stages[stage]
        buf[it, mine] = value
        for peer in peers:
            pltpu.make_async_remote_copy(
                src_ref=buf.at[it, mine],
                dst_ref=buf.at[it, mine],
                send_sem=r_send.at[it, stage],
                recv_sem=r_recv.at[it, stage],
                device_id=peer,
                device_id_type=MESH,
            ).start()

    def part_all(it, stage):
        buf, peers, _ = stages[stage]
        return pltpu.make_async_remote_copy(
            src_ref=buf.at[it, pl.ds(0, len(peers))],
            dst_ref=buf.at[it, pl.ds(0, len(peers))],
            send_sem=r_send.at[it, stage],
            recv_sem=r_recv.at[it, stage],
            device_id=peers[0],
            device_id_type=MESH,
        )

    def send_local(it, sums):
        part_send(it, 0, jnp.sum(sums, axis=0, keepdims=True))

    def send_pair(it):
        part_all(it, 0).wait_recv()
        slots = part_a[it].reshape(nz, 2, 1, steps)
        part_send(it, 1, jnp.sum(slots, axis=0))

    def ratios(it):
        part_all(it, 1).wait_recv()
        fleet = jnp.sum(part_b[it].reshape(nx, ny, 2, steps), axis=0)
        top = jnp.max(fleet, axis=(0, 1, 2), keepdims=True)[0, 0]

        def of(block):
            row = part_b[it, block // 2, lax.rem(block, 2)]
            for k in range(1, nx):
                row = row + part_b[it, k * ny + block // 2, lax.rem(block, 2)]
            return row / top

        return of(tm), of(left[1])

    for load in loads:
        load.start()

    barrier = pltpu.get_barrier_semaphore()
    others = peers_a + peers_b + [left, right]
    for peer in others:
        pl.semaphore_signal(barrier, inc=1, device_id=peer, device_id_type=MESH)

    def fold(value):
        return jnp.sum(value.reshape(value.shape[0] // 8, 8, steps), axis=0)

    sums = jnp.zeros((8, steps), jnp.float32)
    for i in range(2):
        loads[i].wait()
        value = u_now[pl.ds(i * half, half)]
        packed[0, pl.ds(i * half, half)] = value.astype(jnp.bfloat16)
        sums = sums + fold(value)
    sums_first = sums
    for load in loads[3:]:
        load.wait()

    kern = kern_vm[...].astype(jnp.float32)
    gain = gains_vm[...]
    slots = lax.broadcasted_iota(jnp.int32, (zcount, count), 0)
    weight = jnp.where(slots < zones_vm[...], gain, 0.0)
    total = jnp.sum(kern, axis=1, keepdims=True)
    bound = 1.01 * jnp.sum(weight * total * (8.0 + 4.0 * gain * total), axis=0, keepdims=True)
    bound = jnp.maximum(bound, 1e-20)
    scale_in = bound / (CODE * CODE)
    scale_out = (CODE * CODE) / bound
    none = jnp.zeros((6, count), jnp.float32)
    cols[...] = jnp.concatenate([gain, weight, scale_out, scale_in, none], axis=0).T
    nsched = band_low.shape[0]
    plans = lax.broadcasted_iota(jnp.int32, (nsched, count), 0)
    chosen = jnp.where(plans == classes_vm[...], 1.0, 0.0)
    onehot[...] = jnp.concatenate([chosen] * 3, axis=0).T.astype(jnp.bfloat16)

    at_row = lax.broadcasted_iota(jnp.int32, (steps, steps), 0)
    at_col = lax.broadcasted_iota(jnp.int32, (steps, steps), 1)
    edge = jnp.where(tm > 0, 0, steps)
    for slot in range(zcount):
        wide = jnp.broadcast_to(kern[slot : slot + 1], (steps, steps))
        ring = pltpu.roll(wide, 0, 1, stride=1, stride_axis=0)
        place = pl.ds(slot * steps, steps)
        forward[:steps, place] = jnp.where(at_row - at_col > edge, ring, 0.0).astype(jnp.bfloat16)
        forward[steps:, place] = jnp.where(at_row <= at_col, ring, 0.0).astype(jnp.bfloat16)
        ring = ring.T
        adjoint[place, :steps] = jnp.where(at_row >= at_col, ring, 0.0).astype(jnp.bfloat16)
        adjoint[place, steps:] = jnp.where(at_col - at_row > edge, ring, 0.0).astype(jnp.bfloat16)

    pl.semaphore_wait(barrier, len(others))
    spots = list(range(0, count, ROWS))
    for at in spots[:2]:
        u_copy(0, at, ROWS).start()
    send_local(0, sums_first)
    for at in spots[2:LEAD]:
        u_copy(0, at, ROWS).start()

    lows, highs = split3(low_vm[...]), split3(high_vm[...])
    bands = jnp.concatenate(
        [jnp.concatenate([lo, hi], axis=1).astype(jnp.float32) for lo, hi in zip(lows, highs)],
        axis=0,
    ).astype(jnp.bfloat16)
    loads[2].wait()
    for at in range(0, count, half):
        rows = pl.ds(at, half)
        limits = jnp.dot(onehot[rows], bands, preferred_element_type=jnp.float32)
        value = under[rows]
        under[rows] = value - limits[:, :steps]
        over[rows] = value - limits[:, steps:]

    def excess_and_pull(it, at, before):
        rows = pl.ds(at, ROWS)
        col = cols[rows]
        window = jnp.concatenate([before, packed[it, rows]], axis=1)
        hi, lo = over[rows], under[rows]
        parts = []
        for slot in range(zcount):
            place = pl.ds(slot * steps, steps)
            response = jnp.dot(window, forward[:, place], preferred_element_type=jnp.float32)
            change = col[:, slot : slot + 1] * response
            far = jnp.maximum(hi - change, jnp.minimum(lo - change, 0.0))
            scale = col[:, zcount + slot : zcount + slot + 1]
            parts.append((scale * far).astype(jnp.bfloat16))
        excess = jnp.concatenate(parts, axis=1)
        pull = jnp.dot(excess, adjoint[...], preferred_element_type=jnp.float32)
        own[rows] = pull[:, :steps]
        sent = pull[:, steps:]
        length = jnp.sqrt(jnp.abs(sent) * col[:, 2 * zcount : 2 * zcount + 1])
        code = jnp.round(jnp.where(sent < 0.0, -length, length))
        code_out[it, rows] = jnp.clip(code, -CODE, CODE).astype(jnp.int16)
        p_copy(it, at, ROWS).start()

    def free_part(it, at, y_now):
        p_copy(it, at, ROWS).wait_recv()
        rows = pl.ds(at, ROWS)
        code = code_in[it, rows].astype(jnp.float32)
        scale = cols[rows][:, 2 * zcount + 1 : 2 * zcount + 2]
        pull = own[rows] + code * jnp.abs(code) * scale
        return u_now[rows] - 0.5 * (y_now - pull)

    reach = TOP + 0.5
    fine = 2.0 * CODE / reach
    y_now = duals_vm[...]

    def open_first(at):
        u_copy(0, at, ROWS).wait_recv()
        excess_and_pull(0, at, halo_u[pl.ds(at, ROWS)])

    def send_free(at):
        rows = pl.ds(at, ROWS)
        value = free_part(0, at, y_now)
        u_now[rows] = value
        code = jnp.round(jnp.clip(value, 0.0, reach) * fine - CODE)
        free_out[rows] = code.astype(jnp.int16)
        u_copy(1, at, ROWS).start()

    def settle(at, share):
        rows = pl.ds(at, ROWS)
        value = jnp.clip(u_now[rows] - share, 0.0, TOP)
        u_now[rows] = value
        packed[1, rows] = value.astype(jnp.bfloat16)
        return fold(value)

    def open_second(at, share_left):
        u_copy(1, at, ROWS).wait_recv()
        code = free_in[pl.ds(at, ROWS)].astype(jnp.float32)
        before = jnp.clip((code + CODE) * (1.0 / fine) - share_left, 0.0, TOP)
        excess_and_pull(1, at, before.astype(jnp.bfloat16))

    for i, at in enumerate(spots):
        open_first(at)
        if i + LEAD < copies:
            u_copy(0, spots[i + LEAD], ROWS).start()
        if i == 2:
            send_pair(0)
        if i >= LAG:
            send_free(spots[i - LAG])
    send_free(spots[copies - LAG])
    now, now_left = ratios(0)
    share, share_left = 0.5 * now, 0.5 * now_left
    sums = jnp.zeros((8, steps), jnp.float32)
    for at in spots[copies - LAG + 1 :]:
        send_free(at)
        sums = sums + settle(at, share)
    for at in spots[: copies - LAG + 1]:
        sums = sums + settle(at, share)
    send_local(1, sums)
    y_now = y_now + 1.0 * (now - 0.5)

    for at in spots:
        open_second(at, share_left)
    send_pair(1)
    for at in spots:
        own[pl.ds(at, ROWS)] = free_part(1, at, y_now)
    now, _ = ratios(1)
    share = 0.5 * now
    duals_out[...] = y_now + 1.0 * (now - 0.5)
    out[...] = jnp.clip(own[...] - share, 0.0, TOP)

    for it in range(ITERS):
        u_copy(it, 0, count).wait_send()
        p_copy(it, 0, count).wait_send()
        for stage in range(2):
            part_all(it, stage).wait_send()


def body(nz, nx, nt, power, base, band_low, band_high, kernels, gains, zones, classes, duals):
    count, steps = power.shape
    zcount = kernels.shape[0]
    copies = count // ROWS
    nsched = band_low.shape[0]
    vmem = pl.BlockSpec(memory_space=pltpu.VMEM)
    hbm = pl.BlockSpec(memory_space=pltpu.HBM)
    f32, bf16 = jnp.float32, jnp.bfloat16
    whole = pltpu.VMEM((count, steps), f32)
    args = (
        power,
        base,
        band_low,
        band_high,
        kernels,
        gains.T,
        zones[None, :],
        classes[None, :],
        duals[None, :],
    )
    out, duals_out = pl.pallas_call(
        functools.partial(kernel, nz, nx, nt),
        out_shape=(
            jax.ShapeDtypeStruct((count, steps), f32),
            jax.ShapeDtypeStruct((1, steps), f32),
        ),
        in_specs=[hbm] * len(args),
        out_specs=(vmem, vmem),
        scratch_shapes=[pltpu.VMEM(arg.shape, arg.dtype) for arg in args[2:]]
        + [
            whole,
            whole,
            whole,
            whole,
            pltpu.VMEM((ITERS, count, steps), bf16),
            pltpu.VMEM((count, steps), bf16),
            pltpu.VMEM((ITERS, count, steps), jnp.int16),
            pltpu.VMEM((ITERS, count, steps), jnp.int16),
            pltpu.VMEM((count, steps), jnp.int16),
            pltpu.VMEM((count, steps), jnp.int16),
            pltpu.VMEM((2 * steps, zcount * steps), bf16),
            pltpu.VMEM((zcount * steps, 2 * steps), bf16),
            pltpu.VMEM((count, 3 * nsched), bf16),
            pltpu.VMEM((count, 16), f32),
            pltpu.VMEM((ITERS, 2 * nz, 1, steps), f32),
            pltpu.VMEM((ITERS, nx * nt // 2, 2, 1, steps), f32),
            pltpu.SemaphoreType.DMA((3 + len(args) - 2,)),
            pltpu.SemaphoreType.DMA((ITERS,)),
            pltpu.SemaphoreType.DMA((ITERS, copies)),
            pltpu.SemaphoreType.DMA((ITERS,)),
            pltpu.SemaphoreType.DMA((ITERS, copies)),
            pltpu.SemaphoreType.DMA((ITERS, 2)),
            pltpu.SemaphoreType.DMA((ITERS, 2)),
        ],
        compiler_params=pltpu.CompilerParams(
            collective_id=0, has_side_effects=True, vmem_limit_bytes=40 * 1024 * 1024
        ),
    )(*[pltpu.with_memory_space_constraint(arg, pltpu.HBM) for arg in args])
    return out, duals_out[0]


def solution(mesh):
    in_specs = (
        P("bld", "tm"),
        P("bld", "tm"),
        P(None, "tm"),
        P(None, "tm"),
        P(),
        P("bld", None),
        P("bld"),
        P("bld"),
        P("tm"),
    )
    out_specs = (P("bld", "tm"), P("tm"))
    nz = 8 if mesh.shape["bld"] % 8 == 0 else 1
    nx = mesh.shape["bld"] // nz
    return jax.shard_map(
        functools.partial(body, nz, nx, mesh.shape["tm"]),
        mesh=mesh,
        in_specs=in_specs,
        out_specs=out_specs,
        check_vma=False,
    )
```

```python
import functools

import jax
import jax.numpy as jnp
from jax import lax
from jax.experimental import pallas as pl
from jax.experimental.pallas import tpu as pltpu
from jax.sharding import PartitionSpec as P

ITERS = 2
ROWS = 128
MESH = pl.DeviceIdType.MESH
CODE = 32767.0
TOP = 4.0
PIECES = 4
LEAD = 5
LATE = 1
LAG = 5


def split3(value):
    top = value.astype(jnp.bfloat16)
    rest = value - top.astype(jnp.float32)
    mid = rest.astype(jnp.bfloat16)
    low = (rest - mid.astype(jnp.float32)).astype(jnp.bfloat16)
    return [top, mid, low]


def spread(distances):
    return sorted(range(1, len(distances)), key=lambda k: -distances[k])


def around(k, n):
    return min(k, n - k)


def kernel(
    nz,
    nx,
    nt,
    power,
    base,
    band_low,
    band_high,
    kernels,
    gains,
    zones,
    classes,
    duals,
    out,
    duals_out,
    share_out,
    low_vm,
    high_vm,
    kern_vm,
    gains_vm,
    zones_vm,
    classes_vm,
    duals_vm,
    u_now,
    over,
    under,
    own,
    packed,
    halo_u,
    code_out,
    code_in,
    free_out,
    free_in,
    forward,
    adjoint,
    onehot,
    cols,
    part_xt,
    part_z,
    part_zc,
    part_xy,
    load_sem,
    u_send,
    u_recv,
    p_send,
    p_recv,
    r_send,
    r_recv,
):
    count, steps = u_now.shape
    zcount = kernels.shape[0]
    copies = count // ROWS
    ny = nt // 2
    bld = lax.axis_index("bld")
    tm = lax.axis_index("tm")
    x, z = bld // nz, lax.rem(bld, nz)
    y, core = tm // 2, lax.rem(tm, 2)
    right = (bld, lax.rem(tm + 1, nt))
    left = (bld, lax.rem(tm + nt - 1, nt))

    def hops(k):
        return around(k // ny, nx) + around(k % ny, ny)

    far_xt = spread([2 * around(k // nt, nx) + around(k % nt, nt) for k in range(nx * nt)])
    far_z = spread([around(k, nz) for k in range(nz)])
    far_zc = spread([2 * around(k // 2, nz) + k % 2 for k in range(2 * nz)])
    far_xy = spread([hops(k) for k in range(nx * ny)])
    peers_xt = [(lax.rem(x + k // nt, nx) * nz + z, lax.rem(tm + k % nt, nt)) for k in far_xt]
    peers_z = [(x * nz + lax.rem(z + k, nz), tm) for k in far_z]
    peers_zc = [
        (x * nz + lax.rem(z + k // 2, nz), 2 * y + lax.rem(core + k % 2, 2)) for k in far_zc
    ]
    peers_xy = [
        (lax.rem(x + k // ny, nx) * nz + z, 2 * lax.rem(y + k % ny, ny) + core) for k in far_xy
    ]
    stages = (
        ((part_zc, peers_zc, 2 * z + core), (part_xy, peers_xy, x * ny + y)),
        ((part_xt, peers_xt, x * nt + tm), (part_z, peers_z, z)),
    )

    small = (
        (gains, gains_vm),
        (zones, zones_vm),
        (classes, classes_vm),
        (kernels, kern_vm),
        (band_low, low_vm),
        (band_high, high_vm),
        (duals, duals_vm),
    )
    half = count // 2
    piece = count // PIECES
    pieces = [
        pltpu.make_async_copy(
            power.at[pl.ds(i * piece, piece)], u_now.at[pl.ds(i * piece, piece)], load_sem.at[i]
        )
        for i in range(PIECES)
    ]
    base_load = pltpu.make_async_copy(base, under, load_sem.at[PIECES])
    loads = [
        pltpu.make_async_copy(source, target, load_sem.at[PIECES + 1 + i])
        for i, (source, target) in enumerate(small)
    ]

    def u_copy(it, at, size):
        source, target = ((packed.at[0], halo_u), (free_out, free_in))[it]
        return pltpu.make_async_remote_copy(
            src_ref=source.at[pl.ds(at, size)],
            dst_ref=target.at[pl.ds(at, size)],
            send_sem=u_send.at[it],
            recv_sem=u_recv.at[it, at // ROWS],
            device_id=right,
            device_id_type=MESH,
        )

    def p_copy(it, at, size):
        return pltpu.make_async_remote_copy(
            src_ref=code_out.at[it, pl.ds(at, size)],
            dst_ref=code_in.at[it, pl.ds(at, size)],
            send_sem=p_send.at[it],
            recv_sem=p_recv.at[it, at // ROWS],
            device_id=left,
            device_id_type=MESH,
        )

    def part_send(it, stage, value):
        buf, peers, mine = stages[it][stage]
        buf[mine] = value
        for peer in peers:
            pltpu.make_async_remote_copy(
                src_ref=buf.at[mine],
                dst_ref=buf.at[mine],
                send_sem=r_send.at[it, stage],
                recv_sem=r_recv.at[it, stage],
                device_id=peer,
                device_id_type=MESH,
            ).start()

    def part_all(it, stage):
        buf, peers, _ = stages[it][stage]
        return pltpu.make_async_remote_copy(
            src_ref=buf.at[pl.ds(0, len(peers))],
            dst_ref=buf.at[pl.ds(0, len(peers))],
            send_sem=r_send.at[it, stage],
            recv_sem=r_recv.at[it, stage],
            device_id=peers[0],
            device_id_type=MESH,
        )

    def send_local(it, sums):
        part_send(it, 0, jnp.sum(sums, axis=0, keepdims=True))

    def send_rest(it):
        part_all(it, 0).wait_recv()
        buf = stages[it][0][0]
        members, each = ((nz, 2), (nx, nt))[it]
        part_send(it, 1, jnp.sum(buf[...].reshape(members, each, 1, steps), axis=0))

    def ratios(it):
        part_all(it, 1).wait_recv()
        buf = stages[it][1][0]
        if it == 1:
            fleet = jnp.sum(buf[...], axis=0)
            top = jnp.max(fleet, axis=(0, 1, 2), keepdims=True)[0]
        else:
            fleet = jnp.sum(buf[...].reshape(nx, ny, 2, steps), axis=0)
            top = jnp.max(fleet, axis=(0, 1, 2), keepdims=True)[0, 0]

        def of(block):
            if it == 1:
                picks = [buf[k, block] for k in range(nz)]
            else:
                picks = [buf[k * ny + block // 2, lax.rem(block, 2)] for k in range(nx)]
            row = picks[0]
            for pick in picks[1:]:
                row = row + pick
            return row / top

        return of(tm), of(left[1])

    for load in pieces + loads + [base_load]:
        load.start()

    barrier = pltpu.get_barrier_semaphore()
    others = peers_xt + [p for k, p in zip(far_zc, peers_zc) if k > 1]
    for peer in others:
        pl.semaphore_signal(barrier, inc=1, device_id=peer, device_id_type=MESH)

    def fold(value):
        return jnp.sum(value.reshape(value.shape[0] // 8, 8, steps), axis=0)

    spots = list(range(0, count, ROWS))
    sums = jnp.zeros((8, steps), jnp.float32)
    for i, load in enumerate(pieces):
        load.wait()
        rows = pl.ds(i * piece, piece)
        value = u_now[rows]
        packed[0, rows] = value.astype(jnp.bfloat16)
        if i == 0:
            pl.semaphore_wait(barrier, len(others))
        for at in spots[:LEAD]:
            if at // piece == i:
                u_copy(0, at, ROWS).start()
        sums = sums + fold(value)
    send_local(0, sums)
    for load in loads:
        load.wait()

    kern = kern_vm[...].astype(jnp.float32)
    gain = gains_vm[...]
    slots = lax.broadcasted_iota(jnp.int32, (zcount, count), 0)
    weight = jnp.where(slots < zones_vm[...], gain, 0.0)
    total = jnp.sum(kern, axis=1, keepdims=True)
    bound = 1.01 * jnp.sum(weight * total * (8.0 + 4.0 * gain * total), axis=0, keepdims=True)
    bound = jnp.maximum(bound, 1e-20)
    scale_in = bound / (CODE * CODE)
    scale_out = (CODE * CODE) / bound
    none = jnp.zeros((6, count), jnp.float32)
    cols[...] = jnp.concatenate([gain, weight, scale_out, scale_in, none], axis=0).T
    nsched = band_low.shape[0]
    plans = lax.broadcasted_iota(jnp.int32, (nsched, count), 0)
    chosen = jnp.where(plans == classes_vm[...], 1.0, 0.0)
    onehot[...] = jnp.concatenate([chosen] * 3, axis=0).T.astype(jnp.bfloat16)

    at_row = lax.broadcasted_iota(jnp.int32, (steps, steps), 0)
    at_col = lax.broadcasted_iota(jnp.int32, (steps, steps), 1)
    edge = jnp.where(tm > 0, 0, steps)
    for slot in range(zcount):
        wide = jnp.broadcast_to(kern[slot : slot + 1], (steps, steps))
        ring = pltpu.roll(wide, 0, 1, stride=1, stride_axis=0)
        place = pl.ds(slot * steps, steps)
        forward[:steps, place] = jnp.where(at_row - at_col > edge, ring, 0.0).astype(jnp.bfloat16)
        forward[steps:, place] = jnp.where(at_row <= at_col, ring, 0.0).astype(jnp.bfloat16)
        ring = ring.T
        adjoint[place, :steps] = jnp.where(at_row >= at_col, ring, 0.0).astype(jnp.bfloat16)
        adjoint[place, steps:] = jnp.where(at_col - at_row > edge, ring, 0.0).astype(jnp.bfloat16)

    lows, highs = split3(low_vm[...]), split3(high_vm[...])
    bands = jnp.concatenate(
        [jnp.concatenate([lo, hi], axis=1).astype(jnp.float32) for lo, hi in zip(lows, highs)],
        axis=0,
    ).astype(jnp.bfloat16)
    base_load.wait()
    for at in range(0, count, half):
        rows = pl.ds(at, half)
        limits = jnp.dot(onehot[rows], bands, preferred_element_type=jnp.float32)
        value = under[rows]
        under[rows] = value - limits[:, :steps]
        over[rows] = value - limits[:, steps:]

    def excess_and_pull(it, at, before):
        rows = pl.ds(at, ROWS)
        col = cols[rows]
        window = jnp.concatenate([before, packed[it, rows]], axis=1)
        hi, lo = over[rows], under[rows]
        parts = []
        for slot in range(zcount):
            place = pl.ds(slot * steps, steps)
            response = jnp.dot(window, forward[:, place], preferred_element_type=jnp.float32)
            change = col[:, slot : slot + 1] * response
            far = jnp.maximum(hi - change, jnp.minimum(lo - change, 0.0))
            scale = col[:, zcount + slot : zcount + slot + 1]
            parts.append((scale * far).astype(jnp.bfloat16))
        excess = jnp.concatenate(parts, axis=1)
        pull = jnp.dot(excess, adjoint[...], preferred_element_type=jnp.float32)
        own[rows] = pull[:, :steps]
        sent = pull[:, steps:]
        length = jnp.sqrt(jnp.abs(sent) * col[:, 2 * zcount : 2 * zcount + 1])
        code = jnp.round(jnp.where(sent < 0.0, -length, length))
        code_out[it, rows] = jnp.clip(code, -CODE, CODE).astype(jnp.int16)
        p_copy(it, at, ROWS).start()

    def free_part(it, at, y_now):
        p_copy(it, at, ROWS).wait_recv()
        rows = pl.ds(at, ROWS)
        code = code_in[it, rows].astype(jnp.float32)
        scale = cols[rows][:, 2 * zcount + 1 : 2 * zcount + 2]
        pull = own[rows] + code * jnp.abs(code) * scale
        return u_now[rows] - 0.5 * (y_now - pull)

    reach = TOP + 0.5
    fine = 2.0 * CODE / reach
    y_now = duals_vm[...]

    def open_first(at):
        u_copy(0, at, ROWS).wait_recv()
        excess_and_pull(0, at, halo_u[pl.ds(at, ROWS)])

    def send_free(at):
        rows = pl.ds(at, ROWS)
        value = free_part(0, at, y_now)
        u_now[rows] = value
        code = jnp.round(jnp.clip(value, 0.0, reach) * fine - CODE)
        free_out[rows] = code.astype(jnp.int16)
        if at < spots[copies - LATE]:
            u_copy(1, at, ROWS).start()

    def settle(at, share):
        rows = pl.ds(at, ROWS)
        value = jnp.clip(u_now[rows] - share, 0.0, TOP)
        u_now[rows] = value
        packed[1, rows] = value.astype(jnp.bfloat16)
        return fold(value)

    def open_second(at, share_left):
        u_copy(1, at, ROWS).wait_recv()
        code = free_in[pl.ds(at, ROWS)].astype(jnp.float32)
        before = jnp.clip((code + CODE) * (1.0 / fine) - share_left, 0.0, TOP)
        excess_and_pull(1, at, before.astype(jnp.bfloat16))

    for i, at in enumerate(spots):
        open_first(at)
        if i + LEAD < copies:
            u_copy(0, spots[i + LEAD], ROWS).start()
        if i == 2:
            send_rest(0)
        if i >= LAG:
            send_free(spots[i - LAG])
    send_free(spots[copies - LAG])
    now, now_left = ratios(0)
    share, share_left = 0.5 * now, 0.5 * now_left
    sums = jnp.zeros((8, steps), jnp.float32)
    for at in spots[: copies - LAG + 1]:
        sums = sums + settle(at, share)
    for at in spots[copies - LAG + 1 :]:
        send_free(at)
        sums = sums + settle(at, share)
    send_local(1, sums)
    for at in spots[copies - LATE :]:
        u_copy(1, at, ROWS).start()
    y_now = y_now + 1.0 * (now - 0.5)

    for at in spots:
        open_second(at, share_left)
    send_rest(1)
    for at in spots:
        out[pl.ds(at, ROWS)] = free_part(1, at, y_now)
    now, _ = ratios(1)
    duals_out[...] = y_now + 1.0 * (now - 0.5)
    share_out[...] = 0.5 * now

    for it in range(ITERS):
        u_copy(it, 0, count).wait_send()
        p_copy(it, 0, count).wait_send()
        for stage in range(2):
            part_all(it, stage).wait_send()


def body(nz, nx, nt, power, base, band_low, band_high, kernels, gains, zones, classes, duals):
    count, steps = power.shape
    zcount = kernels.shape[0]
    copies = count // ROWS
    nsched = band_low.shape[0]
    vmem = pl.BlockSpec(memory_space=pltpu.VMEM)
    hbm = pl.BlockSpec(memory_space=pltpu.HBM)
    f32, bf16 = jnp.float32, jnp.bfloat16
    whole = pltpu.VMEM((count, steps), f32)
    args = (
        power,
        base,
        band_low,
        band_high,
        kernels,
        gains.T,
        zones[None, :],
        classes[None, :],
        duals[None, :],
    )
    free, duals_out, share = pl.pallas_call(
        functools.partial(kernel, nz, nx, nt),
        out_shape=(
            jax.ShapeDtypeStruct((count, steps), f32),
            jax.ShapeDtypeStruct((1, steps), f32),
            jax.ShapeDtypeStruct((1, steps), f32),
        ),
        in_specs=[hbm] * len(args),
        out_specs=(vmem, vmem, vmem),
        scratch_shapes=[pltpu.VMEM(arg.shape, arg.dtype) for arg in args[2:]]
        + [
            whole,
            whole,
            whole,
            whole,
            pltpu.VMEM((ITERS, count, steps), bf16),
            pltpu.VMEM((count, steps), bf16),
            pltpu.VMEM((ITERS, count, steps), jnp.int16),
            pltpu.VMEM((ITERS, count, steps), jnp.int16),
            pltpu.VMEM((count, steps), jnp.int16),
            pltpu.VMEM((count, steps), jnp.int16),
            pltpu.VMEM((2 * steps, zcount * steps), bf16),
            pltpu.VMEM((zcount * steps, 2 * steps), bf16),
            pltpu.VMEM((count, 3 * nsched), bf16),
            pltpu.VMEM((count, 16), f32),
            pltpu.VMEM((nx * nt, 1, steps), f32),
            pltpu.VMEM((nz, nt, 1, steps), f32),
            pltpu.VMEM((2 * nz, 1, steps), f32),
            pltpu.VMEM((nx * nt // 2, 2, 1, steps), f32),
            pltpu.SemaphoreType.DMA((PIECES + 1 + len(args) - 2,)),
            pltpu.SemaphoreType.DMA((ITERS,)),
            pltpu.SemaphoreType.DMA((ITERS, copies)),
            pltpu.SemaphoreType.DMA((ITERS,)),
            pltpu.SemaphoreType.DMA((ITERS, copies)),
            pltpu.SemaphoreType.DMA((ITERS, 2)),
            pltpu.SemaphoreType.DMA((ITERS, 2)),
        ],
        compiler_params=pltpu.CompilerParams(
            collective_id=0, has_side_effects=True, vmem_limit_bytes=40 * 1024 * 1024
        ),
    )(*[pltpu.with_memory_space_constraint(arg, pltpu.HBM) for arg in args])
    return jnp.clip(free - share, 0.0, TOP), duals_out[0]


def solution(mesh):
    in_specs = (
        P("bld", "tm"),
        P("bld", "tm"),
        P(None, "tm"),
        P(None, "tm"),
        P(),
        P("bld", None),
        P("bld"),
        P("bld"),
        P("tm"),
    )
    out_specs = (P("bld", "tm"), P("tm"))
    nz = 8 if mesh.shape["bld"] % 8 == 0 else 1
    nx = mesh.shape["bld"] // nz
    return jax.shard_map(
        functools.partial(body, nz, nx, mesh.shape["tm"]),
        mesh=mesh,
        in_specs=in_specs,
        out_specs=out_specs,
        check_vma=False,
    )
```

```python
import functools

import jax
import jax.numpy as jnp
from jax import lax
from jax.experimental import pallas as pl
from jax.experimental.pallas import tpu as pltpu
from jax.sharding import PartitionSpec as P

ITERS = 2
ROWS = 128
MESH = pl.DeviceIdType.MESH
CODE = 32767.0
TOP = 4.0
PIECES = 4
LEAD = 5
LATE = 1
LAG = 5


def split3(value):
    top = value.astype(jnp.bfloat16)
    rest = value - top.astype(jnp.float32)
    mid = rest.astype(jnp.bfloat16)
    low = (rest - mid.astype(jnp.float32)).astype(jnp.bfloat16)
    return [top, mid, low]


def spread(distances):
    return sorted(range(1, len(distances)), key=lambda k: -distances[k])


def around(k, n):
    return min(k, n - k)


def kernel(
    nz,
    nx,
    nt,
    power,
    base,
    band_low,
    band_high,
    kernels,
    gains,
    zones,
    classes,
    duals,
    out,
    duals_out,
    share_out,
    low_vm,
    high_vm,
    kern_vm,
    gains_vm,
    zones_vm,
    classes_vm,
    duals_vm,
    u_now,
    over,
    under,
    own,
    packed,
    halo_u,
    code_out,
    code_in,
    free_out,
    free_in,
    forward,
    adjoint,
    onehot,
    cols,
    part_xt,
    part_z,
    part_zc,
    part_xy,
    load_sem,
    u_send,
    u_recv,
    p_send,
    p_recv,
    r_send,
    r_recv,
):
    count, steps = u_now.shape
    zcount = kernels.shape[0]
    copies = count // ROWS
    ny = nt // 2
    bld = lax.axis_index("bld")
    tm = lax.axis_index("tm")
    x, z = bld // nz, lax.rem(bld, nz)
    y, core = tm // 2, lax.rem(tm, 2)
    right = (bld, lax.rem(tm + 1, nt))
    left = (bld, lax.rem(tm + nt - 1, nt))

    def hops(k):
        return around(k // ny, nx) + around(k % ny, ny)

    far_xt = spread([2 * around(k // nt, nx) + around(k % nt, nt) for k in range(nx * nt)])
    far_z = spread([around(k, nz) for k in range(nz)])
    far_zc = spread([2 * around(k // 2, nz) + k % 2 for k in range(2 * nz)])
    far_xy = spread([hops(k) for k in range(nx * ny)])
    peers_xt = [(lax.rem(x + k // nt, nx) * nz + z, lax.rem(tm + k % nt, nt)) for k in far_xt]
    peers_z = [(x * nz + lax.rem(z + k, nz), tm) for k in far_z]
    peers_zc = [
        (x * nz + lax.rem(z + k // 2, nz), 2 * y + lax.rem(core + k % 2, 2)) for k in far_zc
    ]
    peers_xy = [
        (lax.rem(x + k // ny, nx) * nz + z, 2 * lax.rem(y + k % ny, ny) + core) for k in far_xy
    ]
    stages = (
        ((part_zc, peers_zc, 2 * z + core), (part_xy, peers_xy, x * ny + y)),
        ((part_xt, peers_xt, x * nt + tm), (part_z, peers_z, z)),
    )

    small = (
        (gains, gains_vm),
        (zones, zones_vm),
        (classes, classes_vm),
        (kernels, kern_vm),
        (band_low, low_vm),
        (band_high, high_vm),
        (duals, duals_vm),
    )
    half = count // 2
    piece = count // PIECES
    pieces = [
        pltpu.make_async_copy(
            power.at[pl.ds(i * piece, piece)], u_now.at[pl.ds(i * piece, piece)], load_sem.at[i]
        )
        for i in range(PIECES)
    ]
    base_load = pltpu.make_async_copy(base, under, load_sem.at[PIECES])
    loads = [
        pltpu.make_async_copy(source, target, load_sem.at[PIECES + 1 + i])
        for i, (source, target) in enumerate(small)
    ]

    def u_copy(it, at, size):
        source, target = ((packed.at[0], halo_u), (free_out, free_in))[it]
        return pltpu.make_async_remote_copy(
            src_ref=source.at[pl.ds(at, size)],
            dst_ref=target.at[pl.ds(at, size)],
            send_sem=u_send.at[it],
            recv_sem=u_recv.at[it, at // ROWS],
            device_id=right,
            device_id_type=MESH,
        )

    def p_copy(it, at, size):
        return pltpu.make_async_remote_copy(
            src_ref=code_out.at[it, pl.ds(at, size)],
            dst_ref=code_in.at[it, pl.ds(at, size)],
            send_sem=p_send.at[it],
            recv_sem=p_recv.at[it, at // ROWS],
            device_id=left,
            device_id_type=MESH,
        )

    def part_send(it, stage, value):
        buf, peers, mine = stages[it][stage]
        buf[mine] = value
        for peer in peers:
            pltpu.make_async_remote_copy(
                src_ref=buf.at[mine],
                dst_ref=buf.at[mine],
                send_sem=r_send.at[it, stage],
                recv_sem=r_recv.at[it, stage],
                device_id=peer,
                device_id_type=MESH,
            ).start()

    def part_all(it, stage):
        buf, peers, _ = stages[it][stage]
        return pltpu.make_async_remote_copy(
            src_ref=buf.at[pl.ds(0, len(peers))],
            dst_ref=buf.at[pl.ds(0, len(peers))],
            send_sem=r_send.at[it, stage],
            recv_sem=r_recv.at[it, stage],
            device_id=peers[0],
            device_id_type=MESH,
        )

    def send_local(it, sums):
        part_send(it, 0, jnp.sum(sums, axis=0, keepdims=True))

    def send_rest(it):
        part_all(it, 0).wait_recv()
        buf = stages[it][0][0]
        members, each = ((nz, 2), (nx, nt))[it]
        part_send(it, 1, jnp.sum(buf[...].reshape(members, each, 1, steps), axis=0))

    def ratios(it):
        part_all(it, 1).wait_recv()
        buf = stages[it][1][0]
        if it == 1:
            fleet = jnp.sum(buf[...], axis=0)
            top = jnp.max(fleet, axis=(0, 1, 2), keepdims=True)[0]
        else:
            fleet = jnp.sum(buf[...].reshape(nx, ny, 2, steps), axis=0)
            top = jnp.max(fleet, axis=(0, 1, 2), keepdims=True)[0, 0]

        def of(block):
            if it == 1:
                picks = [buf[k, block] for k in range(nz)]
            else:
                picks = [buf[k * ny + block // 2, lax.rem(block, 2)] for k in range(nx)]
            row = picks[0]
            for pick in picks[1:]:
                row = row + pick
            return row / top

        return of(tm), of(left[1])

    for load in pieces + loads + [base_load]:
        load.start()

    barrier = pltpu.get_barrier_semaphore()
    others = peers_xt + [p for k, p in zip(far_zc, peers_zc) if k > 1]
    for peer in others:
        pl.semaphore_signal(barrier, inc=1, device_id=peer, device_id_type=MESH)

    def fold(value):
        return jnp.sum(value.reshape(value.shape[0] // 8, 8, steps), axis=0)

    spots = list(range(0, count, ROWS))
    sums = jnp.zeros((8, steps), jnp.float32)
    for i, load in enumerate(pieces):
        load.wait()
        rows = pl.ds(i * piece, piece)
        value = u_now[rows]
        packed[0, rows] = value.astype(jnp.bfloat16)
        if i == 0:
            pl.semaphore_wait(barrier, len(others))
        for at in spots[:LEAD]:
            if at // piece == i:
                u_copy(0, at, ROWS).start()
        sums = sums + fold(value)
    send_local(0, sums)
    for load in loads:
        load.wait()

    kern = kern_vm[...].astype(jnp.float32)
    gain = gains_vm[...]
    slots = lax.broadcasted_iota(jnp.int32, (zcount, count), 0)
    weight = jnp.where(slots < zones_vm[...], gain, 0.0)
    total = jnp.sum(kern, axis=1, keepdims=True)
    bound = 1.01 * jnp.sum(weight * total * (8.0 + 4.0 * gain * total), axis=0, keepdims=True)
    bound = jnp.maximum(bound, 1e-20)
    scale_in = bound / (CODE * CODE)
    scale_out = (CODE * CODE) / bound
    none = jnp.zeros((6, count), jnp.float32)
    cols[...] = jnp.concatenate([gain, weight, scale_out, scale_in, none], axis=0).T
    nsched = band_low.shape[0]
    plans = lax.broadcasted_iota(jnp.int32, (nsched, count), 0)
    chosen = jnp.where(plans == classes_vm[...], 1.0, 0.0)
    onehot[...] = jnp.concatenate([chosen] * 3, axis=0).T.astype(jnp.bfloat16)

    at_row = lax.broadcasted_iota(jnp.int32, (steps, steps), 0)
    at_col = lax.broadcasted_iota(jnp.int32, (steps, steps), 1)
    edge = jnp.where(tm > 0, 0, steps)
    for slot in range(zcount):
        wide = jnp.broadcast_to(kern[slot : slot + 1], (steps, steps))
        ring = pltpu.roll(wide, 0, 1, stride=1, stride_axis=0)
        place = pl.ds(slot * steps, steps)
        forward[:steps, place] = jnp.where(at_row - at_col > edge, ring, 0.0).astype(jnp.bfloat16)
        forward[steps:, place] = jnp.where(at_row <= at_col, ring, 0.0).astype(jnp.bfloat16)
        ring = ring.T
        adjoint[place, :steps] = jnp.where(at_row >= at_col, ring, 0.0).astype(jnp.bfloat16)
        adjoint[place, steps:] = jnp.where(at_col - at_row > edge, ring, 0.0).astype(jnp.bfloat16)

    lows, highs = split3(low_vm[...]), split3(high_vm[...])
    bands = jnp.concatenate(
        [jnp.concatenate([lo, hi], axis=1).astype(jnp.float32) for lo, hi in zip(lows, highs)],
        axis=0,
    ).astype(jnp.bfloat16)
    base_load.wait()
    for at in range(0, count, half):
        rows = pl.ds(at, half)
        limits = jnp.dot(onehot[rows], bands, preferred_element_type=jnp.float32)
        value = under[rows]
        under[rows] = value - limits[:, :steps]
        over[rows] = value - limits[:, steps:]

    def excess_and_pull(it, at, before, size=ROWS):
        rows = pl.ds(at, size)
        col = cols[rows]
        window = jnp.concatenate([before, packed[it, rows]], axis=1)
        hi, lo = over[rows], under[rows]
        parts = []
        for slot in range(zcount):
            place = pl.ds(slot * steps, steps)
            response = jnp.dot(window, forward[:, place], preferred_element_type=jnp.float32)
            change = col[:, slot : slot + 1] * response
            far = jnp.maximum(hi - change, jnp.minimum(lo - change, 0.0))
            scale = col[:, zcount + slot : zcount + slot + 1]
            parts.append((scale * far).astype(jnp.bfloat16))
        excess = jnp.concatenate(parts, axis=1)
        pull = jnp.dot(excess, adjoint[...], preferred_element_type=jnp.float32)
        own[rows] = pull[:, :steps]
        sent = pull[:, steps:]
        length = jnp.sqrt(jnp.abs(sent) * col[:, 2 * zcount : 2 * zcount + 1])
        code = jnp.round(jnp.where(sent < 0.0, -length, length))
        code_out[it, rows] = jnp.clip(code, -CODE, CODE).astype(jnp.int16)
        for part in range(at, at + size, ROWS):
            p_copy(it, part, ROWS).start()

    def free_part(it, at, y_now):
        p_copy(it, at, ROWS).wait_recv()
        rows = pl.ds(at, ROWS)
        code = code_in[it, rows].astype(jnp.float32)
        scale = cols[rows][:, 2 * zcount + 1 : 2 * zcount + 2]
        pull = own[rows] + code * jnp.abs(code) * scale
        return u_now[rows] - 0.5 * (y_now - pull)

    reach = TOP + 0.5
    fine = 2.0 * CODE / reach
    y_now = duals_vm[...]

    def open_first(at):
        u_copy(0, at, ROWS).wait_recv()
        excess_and_pull(0, at, halo_u[pl.ds(at, ROWS)])

    def send_free(at):
        rows = pl.ds(at, ROWS)
        value = free_part(0, at, y_now)
        u_now[rows] = value
        code = jnp.round(jnp.clip(value, 0.0, reach) * fine - CODE)
        free_out[rows] = code.astype(jnp.int16)
        if at < spots[copies - LATE]:
            u_copy(1, at, ROWS).start()

    def settle(at, share):
        rows = pl.ds(at, ROWS)
        value = jnp.clip(u_now[rows] - share, 0.0, TOP)
        u_now[rows] = value
        packed[1, rows] = value.astype(jnp.bfloat16)
        return fold(value)

    def open_second(at, size, share_left):
        for part in range(at, at + size, ROWS):
            u_copy(1, part, ROWS).wait_recv()
        code = free_in[pl.ds(at, size)].astype(jnp.float32)
        before = jnp.clip((code + CODE) * (1.0 / fine) - share_left, 0.0, TOP)
        excess_and_pull(1, at, before.astype(jnp.bfloat16), size)

    for i, at in enumerate(spots):
        open_first(at)
        if i + LEAD < copies:
            u_copy(0, spots[i + LEAD], ROWS).start()
        if i == 2:
            send_rest(0)
        if i >= LAG:
            send_free(spots[i - LAG])
    send_free(spots[copies - LAG])
    now, now_left = ratios(0)
    share, share_left = 0.5 * now, 0.5 * now_left
    sums = jnp.zeros((8, steps), jnp.float32)
    for at in spots[: copies - LAG + 1]:
        sums = sums + settle(at, share)
    for at in spots[copies - LAG + 1 :]:
        send_free(at)
        sums = sums + settle(at, share)
    send_local(1, sums)
    for at in spots[copies - LATE :]:
        u_copy(1, at, ROWS).start()
    y_now = y_now + 1.0 * (now - 0.5)

    pairs = spots[: copies - 2 : 2]
    for at in pairs:
        open_second(at, 2 * ROWS, share_left)
    for at in spots[copies - 2 :]:
        open_second(at, ROWS, share_left)
    send_rest(1)
    for at in spots:
        out[pl.ds(at, ROWS)] = free_part(1, at, y_now)
    now, _ = ratios(1)
    duals_out[...] = y_now + 1.0 * (now - 0.5)
    share_out[...] = 0.5 * now

    for it in range(ITERS):
        u_copy(it, 0, count).wait_send()
        p_copy(it, 0, count).wait_send()
        for stage in range(2):
            part_all(it, stage).wait_send()


def body(nz, nx, nt, power, base, band_low, band_high, kernels, gains, zones, classes, duals):
    count, steps = power.shape
    zcount = kernels.shape[0]
    copies = count // ROWS
    nsched = band_low.shape[0]
    vmem = pl.BlockSpec(memory_space=pltpu.VMEM)
    hbm = pl.BlockSpec(memory_space=pltpu.HBM)
    f32, bf16 = jnp.float32, jnp.bfloat16
    whole = pltpu.VMEM((count, steps), f32)
    args = (
        power,
        base,
        band_low,
        band_high,
        kernels,
        gains.T,
        zones[None, :],
        classes[None, :],
        duals[None, :],
    )
    free, duals_out, share = pl.pallas_call(
        functools.partial(kernel, nz, nx, nt),
        out_shape=(
            jax.ShapeDtypeStruct((count, steps), f32),
            jax.ShapeDtypeStruct((1, steps), f32),
            jax.ShapeDtypeStruct((1, steps), f32),
        ),
        in_specs=[hbm] * len(args),
        out_specs=(vmem, vmem, vmem),
        scratch_shapes=[pltpu.VMEM(arg.shape, arg.dtype) for arg in args[2:]]
        + [
            whole,
            whole,
            whole,
            whole,
            pltpu.VMEM((ITERS, count, steps), bf16),
            pltpu.VMEM((count, steps), bf16),
            pltpu.VMEM((ITERS, count, steps), jnp.int16),
            pltpu.VMEM((ITERS, count, steps), jnp.int16),
            pltpu.VMEM((count, steps), jnp.int16),
            pltpu.VMEM((count, steps), jnp.int16),
            pltpu.VMEM((2 * steps, zcount * steps), bf16),
            pltpu.VMEM((zcount * steps, 2 * steps), bf16),
            pltpu.VMEM((count, 3 * nsched), bf16),
            pltpu.VMEM((count, 16), f32),
            pltpu.VMEM((nx * nt, 1, steps), f32),
            pltpu.VMEM((nz, nt, 1, steps), f32),
            pltpu.VMEM((2 * nz, 1, steps), f32),
            pltpu.VMEM((nx * nt // 2, 2, 1, steps), f32),
            pltpu.SemaphoreType.DMA((PIECES + 1 + len(args) - 2,)),
            pltpu.SemaphoreType.DMA((ITERS,)),
            pltpu.SemaphoreType.DMA((ITERS, copies)),
            pltpu.SemaphoreType.DMA((ITERS,)),
            pltpu.SemaphoreType.DMA((ITERS, copies)),
            pltpu.SemaphoreType.DMA((ITERS, 2)),
            pltpu.SemaphoreType.DMA((ITERS, 2)),
        ],
        compiler_params=pltpu.CompilerParams(
            collective_id=0, has_side_effects=True, vmem_limit_bytes=40 * 1024 * 1024
        ),
    )(*[pltpu.with_memory_space_constraint(arg, pltpu.HBM) for arg in args])
    return jnp.clip(free - share, 0.0, TOP), duals_out[0]


def solution(mesh):
    in_specs = (
        P("bld", "tm"),
        P("bld", "tm"),
        P(None, "tm"),
        P(None, "tm"),
        P(),
        P("bld", None),
        P("bld"),
        P("bld"),
        P("tm"),
    )
    out_specs = (P("bld", "tm"), P("tm"))
    nz = 8 if mesh.shape["bld"] % 8 == 0 else 1
    nx = mesh.shape["bld"] // nz
    return jax.shard_map(
        functools.partial(body, nz, nx, mesh.shape["tm"]),
        mesh=mesh,
        in_specs=in_specs,
        out_specs=out_specs,
        check_vma=False,
    )
```
